32 devices in a mesh: groups: 2 (over x), sector: 16 (over z, y, core).
Axes of the slice: x: 2, y: 2, z: 4, core: 2. Of those that a mesh axis runs over, the one named last changes fastest.
Arguments:
- wavefunction: bfloat16 [8192, 1024], P(('groups', 'sector')), parts along dimension 0, may hold values from -6 to 6
- widths: int32 [32], P(('groups', 'sector')), parts along dimension 0, may hold values from 1 to 256, 2048 in all
- env_left: bfloat16 [26, 256, 8192], P(None, None, ('groups', 'sector')), parts along dimension 2, may hold values from -0.078125 to 0.078125
- env_right: bfloat16 [52, 64, 64], P('groups'), parts along dimension 0, may hold values from -0.75 to 0.75
- site_tensor: bfloat16 [26, 26, 16, 16], replicated, may hold values from -0.3125 to 0.3125
- shift_class: int32 [26], replicated, may hold values from 0 to 4, as said below
Outputs:
- sigma: bfloat16 [8192, 1024], P(('groups', 'sector')), parts along dimension 0
The draws below stay inside these ranges and needn't reach their ends.
There are 2 independent parts, one for each index of `groups`. The reference program is written for one: setup_inputs(seed, part) draws one part's arguments, and reference() takes and returns one part's arrays. A program takes and returns all parts, laid end to end along the dimension named above; an argument that names none is the same for every part. Nothing has to cross between parts.
Inputs may be any that keep to these rules, and one draw needn't show every extreme that they name: The widths of the 16 sectors sum to 2048, and one of them equals 256. `shift_class`: each class 0 to 4 is held by at least 5 channels.
All inputs are finite; a program needn't handle non-finite values. No bound on the sum of `widths` on one device may be relied on, other than what follows from the above.
Results may differ from the reference program's by a relative error of at most 0.0058.
Values sent between devices are 32-bit elements; how exact they have to be, the bound alone decides.
A program may use at most 192 MiB of HBM per device.

```python
import math
import jax
import jax.numpy as jnp
import numpy as np
from jax import lax

BW = 256
PH = 16
RW = 64
WB = 26
DOWNS = 8
NSEC = 16


def draw_shift_class(key, part):
    key = jax.random.fold_in(key, 7)
    order = jax.random.permutation(key, WB)
    return (order % 5).astype(jnp.int32)


def shard_levels(stream_key, extent, split, low, high):
    factor_of, own = 1.0, jax.random.fold_in(stream_key, 6)
    for axis_at, blocks in split:
        heights = jnp.exp(jax.random.uniform(jax.random.fold_in(own, axis_at), (blocks,), jnp.float32, low / len(split), high / len(split)))
        factor_of = factor_of * jnp.repeat(heights, extent[axis_at] // blocks).reshape([-1 if axis == axis_at else 1 for axis in range(len(extent))])
    return factor_of


def split_up(count, total, limit, slope):
    weights = [(1 << 20) // math.isqrt(rank ** slope) + 1 for rank in range(2, count + 1)]
    rest, holding = total - limit - (count - 1), [1] * (count - 1)
    while rest > 0:
        movable = [i for i in range(count - 1) if holding[i] < limit]
        pool, remaining = sum([weights[i] for i in movable]), rest
        for i in movable:
            extra = min(limit - holding[i], max(1, remaining * weights[i] // pool), rest)
            holding[i] = holding[i] + extra
            rest = rest - extra
    return np.array([limit] + holding)


def uneven_parts(own_key, amount, total, reach, skew):
    if amount == 2:
        one = jax.random.randint(own_key, (), max(1, total - reach), min(reach, total - 1) + 1)
        return jnp.stack([one, total - one])
    lengths = jnp.asarray(split_up(amount, total, reach, skew), jnp.int32)
    couples = (amount - 1) // 2
    giver, receiver = lengths[1:1 + 2 * couples:2], lengths[2:2 + 2 * couples:2]
    margin = jnp.minimum(giver - 1, reach - receiver)
    moved = jax.random.randint(jax.random.fold_in(own_key, 1), (couples,), 0, 1 << 20) % (margin + 1)
    lengths = lengths.at[1:1 + 2 * couples:2].set(giver - moved).at[2:2 + 2 * couples:2].set(receiver + moved)
    return lengths[jax.random.permutation(jax.random.fold_in(own_key, 2), amount)]


def bell_draw(own_key, dims, scale, limit, split=(), kind=jnp.bfloat16):
    factor_of = shard_levels(own_key, dims, split, -0.22, 0.18) if split else 1.0
    array = jax.random.normal(own_key, dims, jnp.float32) * scale * factor_of
    return jnp.minimum(jnp.maximum(array, -limit), limit).astype(kind)


def setup_inputs(seed: int = 0, part: int = 0) -> dict:
    key_list = jax.random.split(jax.random.key(seed), 7)
    part_splits = jax.random.split(jax.random.fold_in(key_list[6], part), 7)
    wavefunction = bell_draw(part_splits[0], (NSEC * BW, PH * RW), 1.0, 6.0, ((0, 16),))
    widths = uneven_parts(part_splits[1], NSEC, NSEC * BW // 2, BW, 2).astype(jnp.int32)
    env_left = bell_draw(part_splits[2], (WB, BW, NSEC * BW), (BW * WB) ** -0.5, 0.078125, ((2, 16),))
    env_right = bell_draw(part_splits[3], (WB, RW, RW), RW ** -0.5, 0.75)
    site_tensor = bell_draw(key_list[4], (WB, WB, PH, PH), (WB * PH) ** -0.5, 0.3125)
    shift_class = draw_shift_class(jax.random.fold_in(key_list[6], 71), part)
    return {"wavefunction": wavefunction, "widths": widths, "env_left": env_left, "env_right": env_right, "site_tensor": site_tensor, "shift_class": shift_class}


def sector_terms(wave_rows, width, env_cols, env_right, site_tensor, class_hot):
    live_rows = (jnp.arange(BW) < width)[:, None]
    live_wave = jnp.where(live_rows, wave_rows, jnp.zeros_like(wave_rows))
    wave_cube = live_wave.reshape(BW, PH, RW).astype(jnp.float32)
    right_applied = jnp.einsum('xsr,vrq->xvsq', wave_cube, env_right.astype(jnp.float32)).astype(jnp.bfloat16)
    site_applied = jnp.einsum('wvts,xvsq->wxtq', site_tensor.astype(jnp.float32), right_applied.astype(jnp.float32)).astype(jnp.bfloat16)
    site_applied = site_applied.reshape(WB, BW, PH * RW)
    return jnp.einsum('wbx,wxc,wk->kbc', env_cols.astype(jnp.float32), site_applied.astype(jnp.float32), class_hot)


def shifted(values, offset):
    pad_block = jnp.zeros((abs(offset),) + values.shape[1:], jnp.float32)
    if offset > 0:
        return jnp.concatenate([pad_block, values[:-offset]], axis=0)
    return jnp.concatenate([values[-offset:], pad_block], axis=0)


def reference(wavefunction, widths, env_left, env_right, site_tensor, shift_class):
    class_hot = (shift_class[:, None] == jnp.arange(5, dtype=jnp.int32)[None, :]).astype(jnp.float32)
    wave_blocks = wavefunction.reshape(NSEC, BW, PH * RW)
    env_blocks = env_left.reshape(WB, BW, NSEC, BW).transpose(2, 0, 1, 3)
    class_terms = lax.map(lambda entry: sector_terms(entry[0], entry[1], entry[2], env_right, site_tensor, class_hot), (wave_blocks, widths, env_blocks))
    sector_ids = jnp.arange(NSEC, dtype=jnp.int32)
    down_index = sector_ids % DOWNS
    raise_part = jnp.where((down_index == DOWNS - 1)[:, None, None], jnp.float32(0.0), class_terms[:, 3])
    lower_part = jnp.where((down_index == 0)[:, None, None], jnp.float32(0.0), class_terms[:, 4])
    summed = class_terms[:, 0] + shifted(class_terms[:, 1], DOWNS) + shifted(class_terms[:, 2], -DOWNS)
    summed = summed + shifted(raise_part, 1) + shifted(lower_part, -1)
    live_rows = jnp.arange(BW)[None, :] < widths[:, None]
    sigma = jnp.where(live_rows[:, :, None], summed, jnp.float32(0.0)).astype(jnp.bfloat16)
    return sigma.reshape(NSEC * BW, PH * RW)
```

```python
import functools

import jax
import jax.numpy as jnp
from jax import lax
from jax.experimental import pallas as pl
from jax.experimental.pallas import tpu as pltpu
from jax.sharding import PartitionSpec as P

DOWNS = 8
CLASSES = 5
CHUNKS = 4
VPAD = 32
MESH = pl.DeviceIdType.MESH
F32 = jnp.float32
BF16 = jnp.bfloat16


def kernel(
    count,
    order_ref,
    width_ref,
    wave_ref,
    envr_ref,
    site_ref,
    env_hbm,
    out_ref,
    env_ref,
    wave_t,
    right_f32,
    right_t,
    mixer,
    right_done,
    site_done,
    terms,
    landed,
    total,
    env_sem,
    send_sem,
    recv_sem,
):
    rows, cols = wave_ref.shape
    channels, _, states, _ = site_ref.shape
    window = envr_ref.shape[1]
    qs = window // CHUNKS
    block = qs * states
    slots = order_ref.shape[0] // (2 * CLASSES)
    me = lax.axis_index("sector")
    down = lax.rem(me, DOWNS)
    offsets = (DOWNS, -DOWNS, 1, -1)
    sends = (me + DOWNS < count, me >= DOWNS, down != DOWNS - 1, down != 0)
    takes = (me >= DOWNS, me + DOWNS < count, down != 0, down != DOWNS - 1)

    env_copy = pltpu.make_async_copy(env_hbm, env_ref, env_sem)
    env_copy.start()
    barrier = pltpu.get_barrier_semaphore()
    for i in range(4):

        @pl.when(sends[i])
        def _():
            pl.semaphore_signal(
                barrier, inc=1, device_id={"sector": me + offsets[i]}, device_id_type=MESH
            )

    live = lax.broadcasted_iota(jnp.int32, (128, rows), 1) < width_ref[0]
    for i in range(cols // 128):
        part = wave_ref[:, i * 128 : (i + 1) * 128].astype(F32).T
        wave_t[i * 128 : (i + 1) * 128, :] = jnp.where(live, part, 0.0).astype(BF16)

    right_f32[...] = jnp.zeros_like(right_f32)
    for v in range(channels):
        flipped = envr_ref[v].astype(F32).T
        wide = jnp.concatenate([flipped, jnp.zeros((window, 128 - window), F32)], axis=1)
        right_f32[pl.ds(v, window, stride=VPAD), :] = wide
    right_t[...] = right_f32[...].astype(BF16)

    depth = states * VPAD
    spot_s = lax.broadcasted_iota(jnp.int32, (states, depth), 0)
    spot_c = lax.broadcasted_iota(jnp.int32, (states, depth), 1)
    packed = jnp.zeros((channels * states, depth), F32)
    for v in range(channels):
        place = (spot_c == spot_s * VPAD + v).astype(F32).astype(BF16)
        packed += jnp.dot(
            site_ref[:, v].reshape(channels * states, states), place, preferred_element_type=F32
        )
    mixer[...] = packed.astype(BF16)

    pl.semaphore_wait(barrier, sum(jnp.where(take, 1, 0) for take in takes))

    def remote(i, c):
        return pltpu.make_async_remote_copy(
            src_ref=terms.at[i, c],
            dst_ref=landed.at[i, c],
            send_sem=send_sem.at[i, c],
            recv_sem=recv_sem.at[i, c],
            device_id={"sector": me + offsets[i]},
            device_id_type=MESH,
        )

    def class_sum(k):
        acc = jnp.zeros((block, rows), F32)
        for j in range(slots):
            at = order_ref[k * slots + j]
            left = env_ref[at]
            if j >= channels // CLASSES:
                held = order_ref[(CLASSES + k) * slots + j].astype(F32)
                left = (left.astype(F32) * held).astype(BF16)
            acc += lax.dot_general(
                site_done[at], left, (((1,), (1,)), ((), ())), preferred_element_type=F32
            )
        return acc

    @pl.loop(0, CHUNKS)
    def _(c):
        right_rows = right_t[pl.ds(pl.multiple_of(c * qs * VPAD, 16), qs * VPAD), :window]
        for s in range(states):
            done = jnp.dot(
                right_rows,
                wave_t[s * window : (s + 1) * window, :],
                preferred_element_type=F32,
            ).astype(BF16)
            right_done[:, s * VPAD : (s + 1) * VPAD, :] = done.reshape(qs, VPAD, rows)
        for q in range(qs):
            done = jnp.dot(mixer[...], right_done[q], preferred_element_type=F32).astype(BF16)
            site_done[:, q * states : (q + 1) * states, :] = done.reshape(channels, states, rows)

        @pl.when(c == 0)
        def _():
            env_copy.wait()

        for i in range(4):

            @pl.when(sends[i])
            def _():
                terms[i, c] = class_sum(i + 1)
                remote(i, c).start()

        own = class_sum(0)
        at = pl.ds(pl.multiple_of(c * block, block), block)
        for h in range(rows // 128):
            total[h, at, :] = own[:, h * 128 : (h + 1) * 128]

    @pl.loop(0, CHUNKS)
    def _(c):
        at = pl.ds(pl.multiple_of(c * block, block), block)
        for i in (2, 3, 0, 1):

            @pl.when(takes[i])
            def _():
                remote(i, c).wait_recv()
                for h in range(rows // 128):
                    total[h, at, :] += landed[i, c, :, h * 128 : (h + 1) * 128]

    per = 128 // window
    for h in range(rows // 128):
        shown = lax.broadcasted_iota(jnp.int32, (128, 128), 0) + h * 128 < width_ref[0]
        for g in range(states // per):
            part = jnp.concatenate(
                [total[h, pl.ds(g * per + e, window, stride=states), :] for e in range(per)], axis=0
            )
            out_ref[h * 128 : (h + 1) * 128, g * 128 : (g + 1) * 128] = jnp.where(
                shown, part.T, 0.0
            ).astype(BF16)

    @pl.loop(0, CHUNKS)
    def _(c):
        for i in range(4):

            @pl.when(sends[i])
            def _():
                remote(i, c).wait_send()


def local(count, wavefunction, widths, env_left, env_right, site_tensor, shift_class):
    rows, cols = wavefunction.shape
    channels = site_tensor.shape[0]
    states = site_tensor.shape[2]
    window = env_right.shape[1]
    slots = channels - (CLASSES - 1) * (channels // CLASSES)
    ids = jnp.arange(channels, dtype=jnp.int32)
    same = shift_class[:, None] == shift_class[None, :]
    ranking = jnp.sum((same & (ids[None, :] < ids[:, None])).astype(jnp.int32), axis=1)
    slot_ids = jnp.arange(CLASSES * slots, dtype=jnp.int32)
    member = (shift_class[None, :] * slots + ranking[None, :] == slot_ids[:, None]).astype(jnp.int32)
    order = jnp.sum(jnp.stack([member * ids[None, :], member]), axis=2).reshape(-1)
    qs = window // CHUNKS
    block = qs * states
    vmem = pl.BlockSpec(memory_space=pltpu.VMEM)
    smem = pl.BlockSpec(memory_space=pltpu.SMEM)
    return pl.pallas_call(
        functools.partial(kernel, count),
        out_shape=jax.ShapeDtypeStruct((rows, cols), BF16),
        in_specs=[smem, smem, vmem, vmem, vmem, pl.BlockSpec(memory_space=pl.ANY)],
        out_specs=vmem,
        scratch_shapes=[
            pltpu.VMEM((channels, rows, rows), BF16),
            pltpu.VMEM((cols, rows), BF16),
            pltpu.VMEM((window * VPAD, 128), F32),
            pltpu.VMEM((window * VPAD, 128), BF16),
            pltpu.VMEM((channels * states, states * VPAD), BF16),
            pltpu.VMEM((qs, states * VPAD, rows), BF16),
            pltpu.VMEM((channels, block, rows), BF16),
            pltpu.VMEM((4, CHUNKS, block, rows), F32),
            pltpu.VMEM((4, CHUNKS, block, rows), F32),
            pltpu.VMEM((rows // 128, cols, 128), F32),
            pltpu.SemaphoreType.DMA,
            pltpu.SemaphoreType.DMA((4, CHUNKS)),
            pltpu.SemaphoreType.DMA((4, CHUNKS)),
        ],
        compiler_params=pltpu.CompilerParams(
            collective_id=0, has_side_effects=True, vmem_limit_bytes=56 * 1024 * 1024
        ),
        cost_estimate=pl.CostEstimate(
            flops=10_000_000_000, bytes_accessed=8_000_000, transcendentals=0
        ),
    )(order, widths, wavefunction, env_right, site_tensor, env_left)


def solution(mesh):
    placed = (
        P(("groups", "sector"), None),
        P(("groups", "sector")),
        P(None, None, ("groups", "sector")),
        P("groups", None, None),
        P(),
        P(),
    )
    return jax.shard_map(
        functools.partial(local, mesh.shape["sector"]),
        mesh=mesh,
        in_specs=placed,
        out_specs=P(("groups", "sector"), None),
        check_vma=False,
    )
```

```python
import functools

import jax
import jax.numpy as jnp
from jax import lax
from jax.experimental import pallas as pl
from jax.experimental.pallas import tpu as pltpu
from jax.sharding import PartitionSpec as P

DOWNS = 8
CLASSES = 5
CHUNKS = 8
VPAD = 32
MESH = pl.DeviceIdType.MESH
F32 = jnp.float32
BF16 = jnp.bfloat16


def kernel(
    count,
    class_ref,
    wave_hbm,
    envr_hbm,
    site_hbm,
    env_hbm,
    width_ref,
    out_ref,
    wave_ref,
    envr_ref,
    site_ref,
    env_ref,
    wave_t,
    right_f32,
    stage,
    mixer,
    right_done,
    site_done,
    terms,
    landed,
    total,
    load_sem,
    send_sem,
    recv_sem,
):
    rows, cols = wave_ref.shape
    channels, states, _, _ = site_ref.shape
    window = envr_ref.shape[1]
    qs = window // CHUNKS
    block = qs * states
    slots = stage.shape[0] // (states * states)
    mixed = slots * states
    me = lax.axis_index("sector")
    down = lax.rem(me, DOWNS)
    offsets = (DOWNS, -DOWNS, 1, -1)
    sends = (me + DOWNS < count, me >= DOWNS, down != DOWNS - 1, down != 0)
    takes = (me >= DOWNS, me + DOWNS < count, down != 0, down != DOWNS - 1)

    loads = [
        pltpu.make_async_copy(source, target, load_sem.at[i])
        for i, (source, target) in enumerate(
            ((wave_hbm, wave_ref), (envr_hbm, envr_ref), (site_hbm, site_ref), (env_hbm, env_ref))
        )
    ]
    for load in loads:
        load.start()
    barrier = pltpu.get_barrier_semaphore()
    for i in range(4):

        @pl.when(sends[i])
        def _():
            pl.semaphore_signal(
                barrier, inc=1, device_id={"sector": me + offsets[i]}, device_id_type=MESH
            )

    def members(k):
        found = [jnp.int32(0)] * slots
        upto = jnp.int32(0)
        for w in range(channels):
            upto = upto + jnp.where(class_ref[w] == k, 1, 0)
            found = [spot + jnp.where(upto <= j, 1, 0) for j, spot in enumerate(found)]
        return found

    order = [members(k) for k in (1, 2, 3, 4, 0)]

    def build_mixer(p):
        for j in range(slots):
            at = jnp.minimum(order[p][j], channels - 1)
            held = jnp.where(order[p][j] < channels, 1.0, 0.0)
            piece = site_ref[at].reshape(states * states, channels).astype(F32) * held
            wide = jnp.concatenate(
                [piece, jnp.zeros((states * states, 128 - channels), F32)], axis=1
            )
            stage[j * states * states : (j + 1) * states * states, :] = wide
        per = 128 // VPAD
        for g in range(states // per):
            part = jnp.concatenate(
                [
                    stage[pl.ds(g * per + e, mixed, stride=states), :][:, :VPAD]
                    for e in range(per)
                ],
                axis=1,
            )
            mixer[p * mixed : (p + 1) * mixed, g * 128 : (g + 1) * 128] = part.astype(BF16)

    def apply_right(c):
        right_rows = right_f32[
            pl.ds(pl.multiple_of(c * qs * VPAD, 16), qs * VPAD), :window
        ].astype(BF16)
        for s in range(states):
            done = jnp.dot(
                right_rows,
                wave_t[s * window : (s + 1) * window, :],
                preferred_element_type=F32,
            ).astype(BF16)
            right_done[:, s * VPAD : (s + 1) * VPAD, :] = done.reshape(qs, VPAD, rows)

    def apply_site(first, last):
        for q in range(qs):
            done = jnp.dot(
                mixer[first * mixed : last * mixed, :], right_done[q], preferred_element_type=F32
            ).astype(BF16)
            site_done[first * slots : last * slots, q * states : (q + 1) * states, :] = (
                done.reshape((last - first) * slots, states, rows)
            )

    def class_sum(p):
        acc = jnp.zeros((block, rows), F32)
        for j in range(slots):
            acc += lax.dot_general(
                site_done[p * slots + j],
                env_ref[jnp.minimum(order[p][j], channels - 1)],
                (((1,), (1,)), ((), ())),
                preferred_element_type=F32,
            )
        return acc

    def remote(i, c):
        return pltpu.make_async_remote_copy(
            src_ref=terms.at[i, c],
            dst_ref=landed.at[i, c],
            send_sem=send_sem.at[i, c],
            recv_sem=recv_sem.at[i, c],
            device_id={"sector": me + offsets[i]},
            device_id_type=MESH,
        )

    def send(i, c):
        terms[i, c] = class_sum(i)
        remote(i, c).start()

    def keep(c):
        own = class_sum(CLASSES - 1)
        at = pl.ds(pl.multiple_of(c * block, block), block)
        for h in range(rows // 128):
            total[h, at, :] = own[:, h * 128 : (h + 1) * 128]

    loads[0].wait()
    live = lax.broadcasted_iota(jnp.int32, (128, rows), 1) < width_ref[0]
    for i in range(cols // 128):
        part = wave_ref[:, i * 128 : (i + 1) * 128].astype(F32).T
        wave_t[i * 128 : (i + 1) * 128, :] = jnp.where(live, part, 0.0).astype(BF16)

    right_f32[...] = jnp.zeros_like(right_f32)
    loads[1].wait()
    for v in range(channels):
        flipped = envr_ref[v].astype(F32).T
        wide = jnp.concatenate([flipped, jnp.zeros((window, 128 - window), F32)], axis=1)
        right_f32[pl.ds(v, window, stride=VPAD), :] = wide
    apply_right(0)

    loads[2].wait()
    loads[3].wait()
    pl.semaphore_wait(barrier, sum(jnp.where(take, 1, 0) for take in takes))
    for i in range(2):

        @pl.when(sends[i])
        def _():
            build_mixer(i)
            apply_site(i, i + 1)
            send(i, 0)

        @pl.when(jnp.logical_not(sends[i]))
        def _():
            mixer[i * mixed : (i + 1) * mixed, :] = jnp.zeros((mixed, mixer.shape[1]), BF16)

    for p in range(2, CLASSES):
        build_mixer(p)
    apply_site(2, CLASSES)
    for i in range(2, 4):

        @pl.when(sends[i])
        def _():
            send(i, 0)

    keep(0)

    @pl.loop(1, CHUNKS)
    def _(c):
        apply_right(c)
        apply_site(0, CLASSES)
        for i in range(4):

            @pl.when(sends[i])
            def _():
                send(i, c)

        keep(c)

    @pl.loop(0, CHUNKS)
    def _(c):
        at = pl.ds(pl.multiple_of(c * block, block), block)
        for i in (2, 3, 0, 1):

            @pl.when(takes[i])
            def _():
                remote(i, c).wait_recv()
                for h in range(rows // 128):
                    total[h, at, :] += landed[i, c, :, h * 128 : (h + 1) * 128]

    per = 128 // window
    for h in range(rows // 128):
        shown = lax.broadcasted_iota(jnp.int32, (128, 128), 0) + h * 128 < width_ref[0]
        for g in range(states // per):
            part = jnp.concatenate(
                [total[h, pl.ds(g * per + e, window, stride=states), :] for e in range(per)], axis=0
            )
            out_ref[h * 128 : (h + 1) * 128, g * 128 : (g + 1) * 128] = jnp.where(
                shown, part.T, 0.0
            ).astype(BF16)

    @pl.loop(0, CHUNKS)
    def _(c):
        for i in range(4):

            @pl.when(sends[i])
            def _():
                remote(i, c).wait_send()


def local(count, wavefunction, widths, env_left, env_right, site_tensor, shift_class):
    rows, cols = wavefunction.shape
    channels = site_tensor.shape[0]
    states = site_tensor.shape[2]
    window = env_right.shape[1]
    slots = channels - (CLASSES - 1) * (channels // CLASSES)
    qs = window // CHUNKS
    block = qs * states
    vmem = pl.BlockSpec(memory_space=pltpu.VMEM)
    smem = pl.BlockSpec(memory_space=pltpu.SMEM)
    anywhere = pl.BlockSpec(memory_space=pl.ANY)
    return pl.pallas_call(
        functools.partial(kernel, count),
        out_shape=jax.ShapeDtypeStruct((rows, cols), BF16),
        in_specs=[smem, anywhere, anywhere, anywhere, anywhere, smem],
        out_specs=vmem,
        scratch_shapes=[
            pltpu.VMEM((rows, cols), BF16),
            pltpu.VMEM((channels, window, window), BF16),
            pltpu.VMEM((channels, states, states, channels), BF16),
            pltpu.VMEM((channels, rows, rows), BF16),
            pltpu.VMEM((cols, rows), BF16),
            pltpu.VMEM((window * VPAD, 128), F32),
            pltpu.VMEM((slots * states * states, 128), F32),
            pltpu.VMEM((CLASSES * slots * states, states * VPAD), BF16),
            pltpu.VMEM((qs, states * VPAD, rows), BF16),
            pltpu.VMEM((CLASSES * slots, block, rows), BF16),
            pltpu.VMEM((4, CHUNKS, block, rows), F32),
            pltpu.VMEM((4, CHUNKS, block, rows), F32),
            pltpu.VMEM((rows // 128, cols, 128), F32),
            pltpu.SemaphoreType.DMA((4,)),
            pltpu.SemaphoreType.DMA((4, CHUNKS)),
            pltpu.SemaphoreType.DMA((4, CHUNKS)),
        ],
        compiler_params=pltpu.CompilerParams(
            collective_id=0, has_side_effects=True, vmem_limit_bytes=56 * 1024 * 1024
        ),
        cost_estimate=pl.CostEstimate(
            flops=10_000_000_000, bytes_accessed=8_000_000, transcendentals=0
        ),
    )(
        shift_class,
        wavefunction,
        env_right,
        site_tensor.transpose(0, 2, 3, 1),
        env_left,
        widths,
    )


def solution(mesh):
    placed = (
        P(("groups", "sector"), None),
        P(("groups", "sector")),
        P(None, None, ("groups", "sector")),
        P("groups", None, None),
        P(),
        P(),
    )
    return jax.shard_map(
        functools.partial(local, mesh.shape["sector"]),
        mesh=mesh,
        in_specs=placed,
        out_specs=P(("groups", "sector"), None),
        check_vma=False,
    )
```

```python
import functools

import jax
import jax.numpy as jnp
from jax import lax
from jax.experimental import pallas as pl
from jax.experimental.pallas import tpu as pltpu
from jax.sharding import PartitionSpec as P

DOWNS = 8
CLASSES = 5
CHUNKS = 8
VPAD = 32
LOADS = 6
MESH = pl.DeviceIdType.MESH
F32 = jnp.float32
BF16 = jnp.bfloat16


def kernel(
    count,
    class_ref,
    wave_hbm,
    envr_hbm,
    site_hbm,
    env_hbm,
    width_ref,
    out_ref,
    wave_ref,
    envr_ref,
    site_ref,
    env_ref,
    wave_t,
    right_f32,
    stage,
    mixer,
    right_done,
    site_done,
    terms,
    landed,
    total,
    load_sem,
    send_sem,
    recv_sem,
):
    rows, cols = wave_ref.shape
    channels, states, _, _ = site_ref.shape
    window = envr_ref.shape[1]
    qs = window // CHUNKS
    block = qs * states
    slots = stage.shape[0] // (states * states)
    mixed = slots * states
    me = lax.axis_index("sector")
    down = lax.rem(me, DOWNS)
    offsets = (DOWNS, -DOWNS, 1, -1)
    sends = (me + DOWNS < count, me >= DOWNS, down != DOWNS - 1, down != 0)
    takes = (me >= DOWNS, me + DOWNS < count, down != 0, down != DOWNS - 1)

    half = channels // 2
    edges = [channels * i // LOADS for i in range(LOADS + 1)]
    pairs = [(wave_hbm, wave_ref), (envr_hbm, envr_ref)]
    for lo, hi in ((0, half), (half, channels)):
        pairs.append((site_hbm.at[lo:hi], site_ref.at[lo:hi]))
    for lo, hi in zip(edges[:-1], edges[1:]):
        pairs.append((env_hbm.at[lo:hi], env_ref.at[lo:hi]))
    loads = [
        pltpu.make_async_copy(source, target, load_sem.at[i])
        for i, (source, target) in enumerate(pairs)
    ]
    for load in loads:
        load.start()
    barrier = pltpu.get_barrier_semaphore()
    for i in range(4):

        @pl.when(sends[i])
        def _():
            pl.semaphore_signal(
                barrier, inc=1, device_id={"sector": me + offsets[i]}, device_id_type=MESH
            )

    def members(k):
        found = [jnp.int32(0)] * slots
        upto = jnp.int32(0)
        for w in range(channels):
            upto = upto + jnp.where(class_ref[w] == k, 1, 0)
            found = [spot + jnp.where(upto <= j, 1, 0) for j, spot in enumerate(found)]
        return found

    order = [members(k) for k in (1, 2, 3, 4, 0)]

    def build_mixer(p):
        for j in range(slots):
            at = jnp.minimum(order[p][j], channels - 1)
            held = jnp.where(order[p][j] < channels, 1.0, 0.0)
            piece = site_ref[at].reshape(states * states, channels).astype(F32) * held
            wide = jnp.concatenate(
                [piece, jnp.zeros((states * states, 128 - channels), F32)], axis=1
            )
            stage[j * states * states : (j + 1) * states * states, :] = wide
        per = 128 // VPAD
        for g in range(states // per):
            part = jnp.concatenate(
                [
                    stage[pl.ds(g * per + e, mixed, stride=states), :][:, :VPAD]
                    for e in range(per)
                ],
                axis=1,
            )
            mixer[p * mixed : (p + 1) * mixed, g * 128 : (g + 1) * 128] = part.astype(BF16)

    def apply_right(c):
        right_rows = right_f32[
            pl.ds(pl.multiple_of(c * qs * VPAD, 16), qs * VPAD), :window
        ].astype(BF16)
        for s in range(states):
            done = jnp.dot(
                right_rows,
                wave_t[s * window : (s + 1) * window, :],
                preferred_element_type=F32,
            ).astype(BF16)
            right_done[:, s * VPAD : (s + 1) * VPAD, :] = done.reshape(qs, VPAD, rows)

    def apply_site(first, last):
        for q in range(qs):
            done = jnp.dot(
                mixer[first * mixed : last * mixed, :], right_done[q], preferred_element_type=F32
            ).astype(BF16)
            site_done[first * slots : last * slots, q * states : (q + 1) * states, :] = (
                done.reshape((last - first) * slots, states, rows)
            )

    def class_sum(p):
        acc = jnp.zeros((block, rows), F32)
        for j in range(slots):
            acc += lax.dot_general(
                site_done[p * slots + j],
                env_ref[jnp.minimum(order[p][j], channels - 1)],
                (((1,), (1,)), ((), ())),
                preferred_element_type=F32,
            )
        return acc

    def remote(i, c):
        return pltpu.make_async_remote_copy(
            src_ref=terms.at[i, c],
            dst_ref=landed.at[i, c],
            send_sem=send_sem.at[i, c],
            recv_sem=recv_sem.at[i, c],
            device_id={"sector": me + offsets[i]},
            device_id_type=MESH,
        )

    def send(i, c):
        terms[i, c] = class_sum(i)
        remote(i, c).start()

    def keep(c):
        own = class_sum(CLASSES - 1)
        at = pl.ds(pl.multiple_of(c * block, block), block)
        for h in range(rows // 128):
            total[h, at, :] = own[:, h * 128 : (h + 1) * 128]

    loads[0].wait()
    live = lax.broadcasted_iota(jnp.int32, (128, rows), 1) < width_ref[0]
    for i in range(cols // 128):
        part = wave_ref[:, i * 128 : (i + 1) * 128].astype(F32).T
        wave_t[i * 128 : (i + 1) * 128, :] = jnp.where(live, part, 0.0).astype(BF16)

    right_f32[...] = jnp.zeros_like(right_f32)
    loads[1].wait()
    for v in range(channels):
        flipped = envr_ref[v].astype(F32).T
        wide = jnp.concatenate([flipped, jnp.zeros((window, 128 - window), F32)], axis=1)
        right_f32[pl.ds(v, window, stride=VPAD), :] = wide
    apply_right(0)

    for load in loads[2:]:
        load.wait()
    pl.semaphore_wait(barrier, sum(jnp.where(take, 1, 0) for take in takes))
    for i in range(2):

        @pl.when(sends[i])
        def _():
            build_mixer(i)
            apply_site(i, i + 1)
            send(i, 0)

        @pl.when(jnp.logical_not(sends[i]))
        def _():
            mixer[i * mixed : (i + 1) * mixed, :] = jnp.zeros((mixed, mixer.shape[1]), BF16)

    for p in range(2, CLASSES):
        build_mixer(p)
    apply_site(2, CLASSES)
    for i in range(2, 4):

        @pl.when(sends[i])
        def _():
            send(i, 0)

    keep(0)

    @pl.loop(1, CHUNKS)
    def _(c):
        apply_right(c)
        apply_site(0, CLASSES)
        for i in range(4):

            @pl.when(sends[i])
            def _():
                send(i, c)

        keep(c)

    @pl.loop(0, CHUNKS)
    def _(c):
        at = pl.ds(pl.multiple_of(c * block, block), block)
        for i in (2, 3, 0, 1):

            @pl.when(takes[i])
            def _():
                remote(i, c).wait_recv()
                for h in range(rows // 128):
                    total[h, at, :] += landed[i, c, :, h * 128 : (h + 1) * 128]

    per = 128 // window
    for h in range(rows // 128):
        shown = lax.broadcasted_iota(jnp.int32, (128, 128), 0) + h * 128 < width_ref[0]
        for g in range(states // per):
            part = jnp.concatenate(
                [total[h, pl.ds(g * per + e, window, stride=states), :] for e in range(per)], axis=0
            )
            out_ref[h * 128 : (h + 1) * 128, g * 128 : (g + 1) * 128] = jnp.where(
                shown, part.T, 0.0
            ).astype(BF16)

    @pl.loop(0, CHUNKS)
    def _(c):
        for i in range(4):

            @pl.when(sends[i])
            def _():
                remote(i, c).wait_send()


def local(count, wavefunction, widths, env_left, env_right, site_tensor, shift_class):
    rows, cols = wavefunction.shape
    channels = site_tensor.shape[0]
    states = site_tensor.shape[2]
    window = env_right.shape[1]
    slots = channels - (CLASSES - 1) * (channels // CLASSES)
    qs = window // CHUNKS
    block = qs * states
    vmem = pl.BlockSpec(memory_space=pltpu.VMEM)
    smem = pl.BlockSpec(memory_space=pltpu.SMEM)
    anywhere = pl.BlockSpec(memory_space=pl.ANY)
    return pl.pallas_call(
        functools.partial(kernel, count),
        out_shape=jax.ShapeDtypeStruct((rows, cols), BF16),
        in_specs=[smem, anywhere, anywhere, anywhere, anywhere, smem],
        out_specs=vmem,
        scratch_shapes=[
            pltpu.VMEM((rows, cols), BF16),
            pltpu.VMEM((channels, window, window), BF16),
            pltpu.VMEM((channels, states, states, channels), BF16),
            pltpu.VMEM((channels, rows, rows), BF16),
            pltpu.VMEM((cols, rows), BF16),
            pltpu.VMEM((window * VPAD, 128), F32),
            pltpu.VMEM((slots * states * states, 128), F32),
            pltpu.VMEM((CLASSES * slots * states, states * VPAD), BF16),
            pltpu.VMEM((qs, states * VPAD, rows), BF16),
            pltpu.VMEM((CLASSES * slots, block, rows), BF16),
            pltpu.VMEM((4, CHUNKS, block, rows), F32),
            pltpu.VMEM((4, CHUNKS, block, rows), F32),
            pltpu.VMEM((rows // 128, cols, 128), F32),
            pltpu.SemaphoreType.DMA((4 + LOADS,)),
            pltpu.SemaphoreType.DMA((4, CHUNKS)),
            pltpu.SemaphoreType.DMA((4, CHUNKS)),
        ],
        compiler_params=pltpu.CompilerParams(
            collective_id=0, has_side_effects=True, vmem_limit_bytes=56 * 1024 * 1024
        ),
        cost_estimate=pl.CostEstimate(
            flops=10_000_000_000, bytes_accessed=8_000_000, transcendentals=0
        ),
    )(
        shift_class,
        wavefunction,
        env_right,
        site_tensor.transpose(0, 2, 3, 1),
        env_left,
        widths,
    )


def solution(mesh):
    placed = (
        P(("groups", "sector"), None),
        P(("groups", "sector")),
        P(None, None, ("groups", "sector")),
        P("groups", None, None),
        P(),
        P(),
    )
    return jax.shard_map(
        functools.partial(local, mesh.shape["sector"]),
        mesh=mesh,
        in_specs=placed,
        out_specs=P(("groups", "sector"), None),
        check_vma=False,
    )
```
